128 devices in a mesh: grp: 64 (over z, y, x), tp: 2 (over core).
Axes of the slice: x: 4, y: 4, z: 4, core: 2. Of those that a mesh axis runs over, the one named last changes fastest.
Arguments:
- context: bfloat16 [65536, 3072], P('grp', 'tp'), may hold values from -6 to 6
- residual: bfloat16 [65536, 6144], P('grp', 'tp')
- out_weight: bfloat16 [3072, 6144], P('tp'), may hold values from -0.15625 to 0.15625
- adapter_down: bfloat16 [3072, 128], P('tp'), may hold values from -0.109375 to 0.109375
- adapter_up: bfloat16 [128, 6144], P(None, 'tp'), may hold values from -0.5 to 0.5
- norm_gain: float32 [6144], P('tp'), may hold values from 0.25 to 1.75
- lengths: int32 [64], P('grp'), may hold values from 1 to 1024
- route_group: int32 [64, 64], P('grp'), may hold values from 0 to 63, as said below
- route_slot: int32 [64, 64], P('grp'), may hold values from 0 to 63, as said below
Outputs:
- policy_rows: bfloat16 [65536, 6144], P('grp', 'tp')
- reference_rows: bfloat16 [65536, 6144], P('grp', 'tp')
The draws below stay inside these ranges and needn't reach their ends.
Inputs may be any that keep to these rules, and one draw needn't show every extreme that they name: Each row of route_group names every learner group exactly once; the two groups of a chosen and rejected pair have equal rows of route_group. `route_slot`: at each learner group the 64 blocks that arrive, one from each group, take the slots 0 to 63 once each; the two blocks of a pair sit in slots 2q and 2q + 1.
All inputs are finite; a program needn't handle non-finite values.
Results may differ from the reference program's by a relative error of at most 0.012.
Values may be sent and summed in bfloat16 or wider, within the bound.
A program may use at most 192 MiB of HBM per device.

```python
import jax
import jax.numpy as jnp
from jax import lax

D = 6144
HC = 3072
RANK = 128
LEN = 1024
HC_DEV = 1536
BLK = 16
ROWS = 65536
N_GRP = 64
N_TP = 2


def pairing_tables(key):
    base = jax.random.fold_in(key, 31)
    key_order, key_paths, key_seats = jax.random.split(base, 3)
    half_count = N_GRP // 2
    shuffled = jax.random.permutation(key_order, N_GRP).astype(jnp.int32)
    position = jnp.zeros((N_GRP,), jnp.int32).at[shuffled].set(jnp.arange(N_GRP, dtype=jnp.int32))
    pair_index = position // 2
    side_index = position % 2
    paths = jax.vmap(lambda subkey: jax.random.permutation(subkey, N_GRP))(jax.random.split(key_paths, half_count)).astype(jnp.int32)
    seats = jax.vmap(lambda subkey: jax.random.permutation(subkey, half_count))(jax.random.split(key_seats, N_GRP)).astype(jnp.int32)
    route_table = paths[pair_index]
    slot_table = 2 * seats[route_table, pair_index[:, None]] + side_index[:, None]
    return (route_table.astype(jnp.int32), slot_table.astype(jnp.int32))


def draw_route_group(key, part):
    return pairing_tables(key)[0]


def draw_route_slot(key, part):
    return pairing_tables(key)[1]


def draw_lengths(key, part):
    base = jax.random.fold_in(key, 53)
    key_values, key_long, key_short = jax.random.split(base, 3)
    values = jax.random.randint(key_values, (N_GRP,), 1, LEN + 1)
    longest = jax.random.randint(key_long, (), 0, N_GRP)
    shortest = (longest + 1 + jax.random.randint(key_short, (), 0, N_GRP - 1)) % N_GRP
    values = values.at[longest].set(LEN).at[shortest].set(1)
    return values.astype(jnp.int32)


def draw_residual(key, part):
    base = jax.random.fold_in(key, 47)
    key_noise, key_rows, key_cols = jax.random.split(base, 3)
    column = jnp.arange(D, dtype=jnp.float32) / D
    column_scale = 10.0 ** (0.7 * column + 0.5 * jax.random.uniform(key_cols, (D,), dtype=jnp.float32) - 0.6)
    row_scale = 10.0 ** (0.6 * jax.random.uniform(key_rows, (ROWS, 1), dtype=jnp.float32) - 0.3)
    noise = jax.random.normal(key_noise, (ROWS, D), dtype=jnp.float32)
    return (noise * row_scale * column_scale[None, :]).astype(jnp.bfloat16)


def spiked(entries, own_key, source, target, shards_of, factor):
    owner, partner = [(jnp.arange(entries.shape[axis_at]) // (entries.shape[axis_at] // shards_of)).reshape([-1 if axis == axis_at else 1 for axis in range(entries.ndim)]) for axis_at in (source, target)]
    chosen = jax.random.permutation(own_key, shards_of)[partner]
    strong = (owner == chosen) | (owner == (partner + shards_of // 2) % shards_of)
    return jnp.where(strong, factor * entries, entries)


def block_scale(key, extent, pieces, low, top_value):
    loudness = 1.0
    for dim, parts in pieces:
        heights = jax.random.uniform(jax.random.fold_in(jax.random.fold_in(key, 6), dim), (parts,), jnp.float32, low / len(pieces), top_value / len(pieces))
        loudness = loudness * jnp.repeat(jnp.exp(heights), extent[dim] // parts).reshape((-1,) + (1,) * (len(extent) - 1 - dim))
    return loudness


def bell_draw(key, extent, width, bound, cuts=(), kind=jnp.bfloat16):
    factor_of = block_scale(key, extent, cuts, -0.22, 0.18) if cuts else 1.0
    array = jax.random.normal(key, extent, jnp.float32) * width * factor_of
    return jnp.minimum(jnp.maximum(array, -bound), bound).astype(kind)


def gaussian_with(rng, extent, scale, reach, shards, heavy, kind=jnp.bfloat16):
    result = scale * jax.random.normal(rng, extent, jnp.float32)
    if shards:
        result = result * block_scale(rng, extent, shards, -0.22, 0.18)
    return jnp.clip(spiked(result, jax.random.fold_in(rng, 3), *heavy), -reach, reach).astype(kind)


def setup_inputs(seed: int = 0) -> dict:
    splits = jax.random.split(jax.random.key(seed), 10)
    context = bell_draw(splits[0], (ROWS, HC), 1.0, 6.0, ((0, 64), (1, 2)))
    residual = draw_residual(jax.random.fold_in(splits[9], 71), 0)
    out_weight = gaussian_with(splits[2], (HC, D), HC ** -0.5, 0.15625, ((0, 2),), (0, 1, 2, 2.0))
    adapter_down = bell_draw(splits[3], (HC, RANK), HC ** -0.5, 0.109375, ((0, 2),))
    adapter_up = bell_draw(splits[4], (RANK, D), RANK ** -0.5, 0.5, ((1, 2),))
    norm_gain = jnp.clip(1.0 + 0.15 * jax.random.normal(splits[5], (D,), jnp.float32), 0.25, 1.75)
    lengths = draw_lengths(jax.random.fold_in(splits[9], 71), 0)
    route_group = draw_route_group(jax.random.fold_in(splits[9], 71), 0)
    route_slot = draw_route_slot(jax.random.fold_in(splits[9], 71), 0)
    return dict(context=context, residual=residual, out_weight=out_weight, adapter_down=adapter_down, adapter_up=adapter_up, norm_gain=norm_gain, lengths=lengths, route_group=route_group, route_slot=route_slot)


EPSILON = 1e-05

def reference(context, residual, out_weight, adapter_down, adapter_up, norm_gain, lengths, route_group, route_slot):
    blocks = N_GRP
    source = jnp.arange(blocks * blocks, dtype=jnp.int32)
    target = (route_group * blocks + route_slot).reshape(-1).astype(jnp.int32)
    inverse = jnp.zeros((blocks * blocks,), jnp.int32).at[target].set(source)
    starts = jnp.arange(blocks, dtype=jnp.int32) * BLK
    valid_count = jnp.clip(lengths[:, None] - starts[None, :], 0, BLK).reshape(-1).astype(jnp.int32)
    moved_valid = valid_count[inverse].reshape(N_GRP, blocks)
    moved_context = context.reshape(blocks * blocks, BLK, HC)[inverse].reshape(N_GRP, LEN, HC)
    moved_residual = residual.reshape(blocks * blocks, BLK, D)[inverse].reshape(N_GRP, LEN, D)
    weight = out_weight.astype(jnp.float32).reshape(N_TP, HC_DEV, D)
    gain_row = norm_gain.astype(jnp.float32)[None, :]
    token_index = jnp.arange(BLK, dtype=jnp.int32)

    def one_group(group_item):
        context_rows, residual_rows, valid_here = group_item
        partials = jnp.einsum('rjk,jkd->jrd', context_rows.astype(jnp.float32).reshape(LEN, N_TP, HC_DEV), weight)
        rounded = lax.optimization_barrier(partials.astype(jnp.bfloat16))
        attention = lax.optimization_barrier(jnp.sum(rounded.astype(jnp.float32), axis=0))
        adapter_in = jnp.dot(context_rows, adapter_down, preferred_element_type=jnp.float32).astype(jnp.bfloat16)
        reference_hidden = residual_rows.astype(jnp.float32) + attention
        policy_hidden = reference_hidden + jnp.dot(adapter_in, adapter_up, preferred_element_type=jnp.float32)
        live_rows = (token_index[None, :] < valid_here[:, None]).reshape(LEN).astype(jnp.float32)[:, None]

        def normed(hidden):
            mean_square = lax.optimization_barrier(jnp.mean(hidden * hidden, axis=-1, keepdims=True))
            return (hidden * lax.rsqrt(mean_square + EPSILON) * gain_row * live_rows).astype(jnp.bfloat16)
        return (normed(policy_hidden), normed(reference_hidden))
    policy_out, reference_out = lax.map(one_group, (moved_context, moved_residual, moved_valid))
    return (policy_out.reshape(ROWS, D), reference_out.reshape(ROWS, D))
```

```python
import functools

import jax
import jax.numpy as jnp
from jax import lax
from jax.experimental import pallas as pl
from jax.experimental.pallas import tpu as pltpu
from jax.sharding import PartitionSpec as P

EPSILON = 1e-05
MESH = pl.DeviceIdType.MESH

GROUPS = 64
SIDE = 4
BLK = 16
ROWS = 1024
KDIM = 1536
HALF = 3072
FULL = 6144
RANK = 128
PER = 16
MB = PER * BLK
NB = GROUPS // PER
CW = 512
NC = HALF // CW
MSG = HALF + RANK


def send_offsets():
    def distance(o):
        return sum(min(v, SIDE - v) for v in o)

    every = [(z, y, x) for z in range(SIDE) for y in range(SIDE) for x in range(SIDE)]
    every.remove((0, 0, 0))
    order = []
    for o in sorted(every, key=distance):
        for turn in (o, (o[1], o[2], o[0]), (o[2], o[0], o[1])):
            for w in (turn, tuple((SIDE - v) % SIDE for v in turn)):
                if w not in order:
                    order.append(w)
    order.append((0, 0, 0))
    return [(z * SIDE + y) * SIDE + x for z, y, x in order]


def packed_offsets():
    codes = send_offsets() + [0]
    return [sum(codes[5 * w + e] << (6 * e) for e in range(5)) for w in range(13)]


def target(j, me):
    word_at, lane = j // 5, j % 5
    word = jnp.int32(0)
    for index, value in enumerate(packed_offsets()):
        word = jnp.where(word_at == index, jnp.int32(value), word)
    code = (word >> (6 * lane)) & 63
    result = jnp.int32(0)
    for unit in (16, 4, 1):
        step = (code // unit) % SIDE
        result = result + ((me // unit) % SIDE + step) % SIDE * unit
    return result


def route_kernel(
    meta,
    ctx_hbm,
    res_hbm,
    w_hbm,
    down_hbm,
    up_hbm,
    gain_hbm,
    rows_out,
    aux_out,
    ctx_v,
    res_v,
    w_v,
    down_v,
    up_v,
    gain_v,
    lhs,
    own,
    hid,
    xs,
    xr,
    a_send,
    a_recv,
    a_full,
    s_send,
    s_recv,
    msg,
    aux,
    load_sem,
    w_sem,
    xs_sem,
    xr_sem,
    as_sem,
    ar_sem,
    ss_sem,
    sr_sem,
    ms_sem,
    mr_sem,
    us_sem,
    ur_sem,
):
    me = lax.axis_index("grp")
    tp = lax.axis_index("tp")
    mate = 1 - tp

    barrier = pltpu.get_barrier_semaphore()

    def greet(i, carry):
        pl.semaphore_signal(
            barrier, inc=1, device_id=((me + i) % GROUPS, tp), device_id_type=MESH
        )
        return carry

    loads = [
        pltpu.make_async_copy(ctx_hbm, ctx_v, load_sem.at[0]),
        pltpu.make_async_copy(down_hbm, down_v, load_sem.at[1]),
        pltpu.make_async_copy(res_hbm, res_v, load_sem.at[2]),
        pltpu.make_async_copy(up_hbm, up_v, load_sem.at[3]),
        pltpu.make_async_copy(gain_hbm, gain_v, load_sem.at[4]),
    ]

    def weight_load(c):
        half = jnp.where(c < NC, mate, tp)
        start = pl.multiple_of(half * HALF + (c % NC) * CW, CW)
        return pltpu.make_async_copy(w_hbm.at[:, pl.ds(start, CW)], w_v.at[c], w_sem.at[c])

    def mate_copy(src, dst, ssem, rsem):
        return pltpu.make_async_remote_copy(
            src_ref=src,
            dst_ref=dst,
            send_sem=ssem,
            recv_sem=rsem,
            device_id=(me, mate),
            device_id_type=MESH,
        )

    def half_copy(k, c):
        return mate_copy(xs.at[k, c], xr.at[k, c], xs_sem.at[k, c], xr_sem.at[k, c])

    def adapter_copy(k):
        return mate_copy(a_send.at[k], a_recv.at[k], as_sem.at[k], ar_sem.at[k])

    def square_copy(k):
        return mate_copy(s_send.at[k], s_recv.at[k], ss_sem.at[k], sr_sem.at[k])

    def row_copy(j, there, slot):
        return pltpu.make_async_remote_copy(
            src_ref=msg.at[j],
            dst_ref=rows_out.at[slot],
            send_sem=ms_sem.at[j],
            recv_sem=mr_sem.at[slot],
            device_id=(there, tp),
            device_id_type=MESH,
        )

    def aux_copy(j, there, slot):
        return pltpu.make_async_remote_copy(
            src_ref=aux.at[j],
            dst_ref=aux_out.at[slot],
            send_sem=us_sem.at[j],
            recv_sem=ur_sem.at[slot],
            device_id=(there, tp),
            device_id_type=MESH,
        )

    loads[0].start()
    loads[1].start()

    def start_weight(c, carry):
        weight_load(c).start()
        return carry

    lax.fori_loop(0, 2 * NC, start_weight, 0)
    for copy in loads[2:]:
        copy.start()

    lax.fori_loop(1, GROUPS, greet, 0)
    pl.semaphore_signal(barrier, inc=1, device_id=(me, mate), device_id_type=MESH)
    loads[0].wait()
    loads[1].wait()
    pl.semaphore_wait(barrier, GROUPS)

    lane = lax.broadcasted_iota(jnp.int32, (BLK, RANK), 1)
    token = lax.broadcasted_iota(jnp.int32, (BLK, RANK), 0)
    live_count = meta[2 * GROUPS]

    def batch(k, carry):
        def gather(i, c):
            there = target(k * PER + i, me)
            lhs[i] = ctx_v[meta[there]]
            return c

        lax.fori_loop(0, PER, gather, 0)
        a_send[k] = jnp.dot(
            lhs[...].reshape(MB, KDIM), down_v[...], preferred_element_type=jnp.float32
        )
        adapter_copy(k).start()

        def away(c, carry2):
            @pl.when(k == 0)
            def _():
                weight_load(c).wait()

            xs[k, c] = jnp.dot(
                lhs[...].reshape(MB, KDIM), w_v[c], preferred_element_type=jnp.float32
            ).astype(jnp.bfloat16)
            half_copy(k, c).start()
            return carry2

        lax.fori_loop(0, NC, away, 0)

        def home(c, carry2):
            @pl.when(k == 0)
            def _():
                weight_load(NC + c).wait()

            own[c] = jnp.dot(
                lhs[...].reshape(MB, KDIM), w_v[NC + c], preferred_element_type=jnp.float32
            ).astype(jnp.bfloat16)
            return carry2

        lax.fori_loop(0, NC, home, 0)

        @pl.when(k == 0)
        def _():
            for copy in loads[2:]:
                copy.wait()

        adapter_copy(k).wait_recv()
        a_full[...] = (a_send[k] + a_recv[k]).astype(jnp.bfloat16)

        def lift(c, carry2):
            cols = pl.ds(pl.multiple_of(c * CW, CW), CW)
            hid[c] = jnp.dot(a_full[...], up_v[:, cols], preferred_element_type=jnp.float32)
            return carry2

        lax.fori_loop(0, NC, lift, 0)

        def arrive(c, carry2):
            half_copy(k, c).wait_recv()
            return carry2

        lax.fori_loop(0, NC, arrive, 0)

        def squares(i, carry2):
            block = meta[target(k * PER + i, me)]
            at = pl.ds(pl.multiple_of(i * BLK, BLK), BLK)
            ref_sum = jnp.zeros((BLK, CW), jnp.float32)
            pol_sum = jnp.zeros((BLK, CW), jnp.float32)
            for c in range(NC):
                h = (
                    own[c, at, :].astype(jnp.float32)
                    + xr[k, c, at, :].astype(jnp.float32)
                    + res_v[block, :, c * CW : (c + 1) * CW].astype(jnp.float32)
                )
                q = h + hid[c, at, :]
                hid[c, at, :] = h
                ref_sum = ref_sum + h * h
                pol_sum = pol_sum + q * q
            s_send[k, at, :] = jnp.where(
                lane < RANK // 2,
                jnp.sum(ref_sum, axis=1, keepdims=True),
                jnp.sum(pol_sum, axis=1, keepdims=True),
            )
            return carry2

        lax.fori_loop(0, PER, squares, 0)
        square_copy(k).start()
        square_copy(k).wait_recv()

        def finish(i, carry2):
            j = k * PER + i
            there = target(j, me)
            block = meta[there]
            at = pl.ds(pl.multiple_of(i * BLK, BLK), BLK)
            total = s_send[k, at, :] + s_recv[k, at, :]
            live = jnp.where(block * BLK + token < live_count, 1.0, 0.0)
            scale = lax.rsqrt(total / FULL + EPSILON) * live
            ref_scale = scale[:, 0:1]
            pol_scale = scale[:, RANK // 2 : RANK // 2 + 1]
            unmasked = lax.rsqrt(total / FULL + EPSILON)
            ratio = pol_scale / unmasked[:, 0:1]
            for c in range(NC):
                cols = slice(c * CW, (c + 1) * CW)
                msg[j, :, cols] = (hid[c, at, :] * ref_scale * gain_v[:, cols]).astype(
                    jnp.bfloat16
                )
            msg[j, :, HALF:] = a_full[at, :]
            line = jnp.where(
                lane == token, ratio, jnp.where(lane == token + BLK, pol_scale, 0.0)
            )
            seat = jnp.where(
                (token == 0) & (lane == 2 * BLK),
                meta[GROUPS + there].astype(jnp.float32),
                0.0,
            )
            aux[j] = jnp.sum(line + seat, axis=0, keepdims=True)

            @pl.when(j < GROUPS - 1)
            def _():
                row_copy(j, there, me).start()
                aux_copy(j, there, me).start()

            return carry2

        lax.fori_loop(0, PER, finish, 0)
        return carry

    lax.fori_loop(0, NB, batch, 0)

    keep_rows = pltpu.make_async_copy(msg.at[GROUPS - 1], rows_out.at[me], load_sem.at[0])
    keep_aux = pltpu.make_async_copy(aux.at[GROUPS - 1], aux_out.at[me], load_sem.at[1])
    keep_rows.start()
    keep_aux.start()

    def drain_mate(k, carry):
        adapter_copy(k).wait_send()
        square_copy(k).wait_send()

        def drain_half(c, carry2):
            half_copy(k, c).wait_send()
            return carry2

        lax.fori_loop(0, NC, drain_half, 0)
        return carry

    lax.fori_loop(0, NB, drain_mate, 0)
    keep_rows.wait()
    keep_aux.wait()

    def drain(i, carry):
        source = (me + i) % GROUPS
        aux_copy(i - 1, source, source).wait()
        row_copy(i - 1, source, source).wait()
        return carry

    lax.fori_loop(1, GROUPS, drain, 0)


def route(meta, context, residual, out_weight, adapter_down, adapter_up, gain):
    any_space = pl.BlockSpec(memory_space=pl.ANY)
    dma = pltpu.SemaphoreType.DMA
    bf16, f32 = jnp.bfloat16, jnp.float32
    return pl.pallas_call(
        route_kernel,
        out_shape=(
            jax.ShapeDtypeStruct((GROUPS, BLK, MSG), bf16),
            jax.ShapeDtypeStruct((GROUPS, 1, RANK), f32),
        ),
        in_specs=[pl.BlockSpec(memory_space=pltpu.SMEM)] + [any_space] * 6,
        out_specs=(any_space, any_space),
        scratch_shapes=[
            pltpu.VMEM((GROUPS, BLK, KDIM), bf16),
            pltpu.VMEM((GROUPS, BLK, HALF), bf16),
            pltpu.VMEM((2 * NC, KDIM, CW), bf16),
            pltpu.VMEM((KDIM, RANK), bf16),
            pltpu.VMEM((RANK, HALF), bf16),
            pltpu.VMEM((1, HALF), f32),
            pltpu.VMEM((PER, BLK, KDIM), bf16),
            pltpu.VMEM((NC, MB, CW), bf16),
            pltpu.VMEM((NC, MB, CW), f32),
            pltpu.VMEM((NB, NC, MB, CW), bf16),
            pltpu.VMEM((NB, NC, MB, CW), bf16),
            pltpu.VMEM((NB, MB, RANK), f32),
            pltpu.VMEM((NB, MB, RANK), f32),
            pltpu.VMEM((MB, RANK), bf16),
            pltpu.VMEM((NB, MB, RANK), f32),
            pltpu.VMEM((NB, MB, RANK), f32),
            pltpu.VMEM((GROUPS, BLK, MSG), bf16),
            pltpu.VMEM((GROUPS, 1, RANK), f32),
            dma((5,)),
            dma((2 * NC,)),
            dma((NB, NC)),
            dma((NB, NC)),
            dma((NB,)),
            dma((NB,)),
            dma((NB,)),
            dma((NB,)),
            dma((GROUPS,)),
            dma((GROUPS,)),
            dma((GROUPS,)),
            dma((GROUPS,)),
        ],
        compiler_params=pltpu.CompilerParams(
            collective_id=0, has_side_effects=True, vmem_limit_bytes=60 * 2**20
        ),
        cost_estimate=pl.CostEstimate(
            flops=2 * ROWS * KDIM * FULL, bytes_accessed=48 * 2**20, transcendentals=0
        ),
        name="route",
    )(meta, context, residual, out_weight, adapter_down, adapter_up, gain)


OUT_PER = 8


def place_kernel(sources, *refs):
    rows = refs[:OUT_PER]
    lines = refs[OUT_PER : 2 * OUT_PER]
    up, gain, policy, reference, inner = refs[2 * OUT_PER :]
    for e in range(OUT_PER):
        inner[e * BLK : (e + 1) * BLK, :] = rows[e][0, :, HALF:]
    lane = lax.broadcasted_iota(jnp.int32, (BLK, RANK), 1)
    token = lax.broadcasted_iota(jnp.int32, (BLK, RANK), 0)
    scales = []
    for e in range(OUT_PER):
        line = jnp.broadcast_to(lines[e][0], (BLK, RANK))
        scales.append(
            (
                jnp.sum(jnp.where(lane == token, line, 0.0), axis=1, keepdims=True),
                jnp.sum(jnp.where(lane == token + BLK, line, 0.0), axis=1, keepdims=True),
            )
        )
    for c in range(NC):
        cols = slice(c * CW, (c + 1) * CW)
        delta = jnp.dot(inner[...], up[:, cols], preferred_element_type=jnp.float32)
        for e in range(OUT_PER):
            at = slice(e * BLK, (e + 1) * BLK)
            ratio, pol_scale = scales[e]
            ref_rows = rows[e][0, :, cols]
            reference[at, cols] = ref_rows
            policy[at, cols] = (
                ref_rows.astype(jnp.float32) * ratio
                + delta[at, :] * pol_scale * gain[:, cols]
            ).astype(jnp.bfloat16)


def place(sources, rows, lines, adapter_up, gain):
    def block_at(e):
        return lambda i, table: (table[i * OUT_PER + e], 0, 0)

    whole = lambda i, table: (0, 0)
    out_spec = pl.BlockSpec((OUT_PER * BLK, HALF), lambda i, table: (i, 0))
    return pl.pallas_call(
        place_kernel,
        grid_spec=pltpu.PrefetchScalarGridSpec(
            num_scalar_prefetch=1,
            grid=(GROUPS // OUT_PER,),
            in_specs=[pl.BlockSpec((1, BLK, MSG), block_at(e)) for e in range(OUT_PER)]
            + [pl.BlockSpec((1, 1, RANK), block_at(e)) for e in range(OUT_PER)]
            + [pl.BlockSpec((RANK, HALF), whole), pl.BlockSpec((1, HALF), whole)],
            out_specs=[out_spec, out_spec],
            scratch_shapes=[pltpu.VMEM((OUT_PER * BLK, RANK), jnp.bfloat16)],
        ),
        out_shape=[jax.ShapeDtypeStruct((ROWS, HALF), jnp.bfloat16)] * 2,
        compiler_params=pltpu.CompilerParams(vmem_limit_bytes=48 * 2**20),
        name="place",
    )(sources, *([rows] * OUT_PER), *([lines] * OUT_PER), adapter_up, gain)


def local(
    context,
    residual,
    out_weight,
    adapter_down,
    adapter_up,
    norm_gain,
    lengths,
    route_group,
    route_slot,
):
    position = jnp.arange(GROUPS, dtype=jnp.int32)
    chosen = route_group[0][None, :] == position[:, None]
    block_for = jnp.sum(jnp.where(chosen, position[None, :], 0), axis=1)
    seat_for = jnp.sum(jnp.where(chosen, route_slot[0][None, :], 0), axis=1)
    meta = jnp.concatenate([block_for, seat_for, lengths]).astype(jnp.int32)
    gain = norm_gain[None, :]
    rows, lines = route(
        meta,
        context.reshape(GROUPS, BLK, KDIM),
        residual.reshape(GROUPS, BLK, HALF),
        out_weight,
        adapter_down,
        adapter_up,
        gain,
    )
    seats = lines[:, 0, 2 * BLK].astype(jnp.int32)
    sources = jnp.sum(
        jnp.where(seats[None, :] == position[:, None], position[None, :], 0), axis=1
    ).astype(jnp.int32)
    return tuple(place(sources, rows, lines, adapter_up, gain))


def solution(mesh):
    in_specs = (
        P("grp", "tp"),
        P("grp", "tp"),
        P("tp", None),
        P("tp", None),
        P(None, "tp"),
        P("tp"),
        P("grp"),
        P("grp", None),
        P("grp", None),
    )
    out_specs = (P("grp", "tp"), P("grp", "tp"))
    return jax.shard_map(local, mesh=mesh, in_specs=in_specs, out_specs=out_specs, check_vma=False)
```

```python
import functools

import jax
import jax.numpy as jnp
from jax import lax
from jax.experimental import pallas as pl
from jax.experimental.pallas import tpu as pltpu
from jax.sharding import PartitionSpec as P

EPSILON = 1e-05
MESH = pl.DeviceIdType.MESH

GROUPS = 64
SIDE = 4
BLK = 16
ROWS = 1024
KDIM = 1536
HALF = 3072
FULL = 6144
RANK = 128
PER = 16
MB = PER * BLK
NR = GROUPS // PER
CW = 512
NC = HALF // CW
UNITS = NC * NR
RING = 4
WRING = 4


def send_offsets():
    def distance(o):
        return sum(min(v, SIDE - v) for v in o)

    def negative(o):
        return tuple((SIDE - v) % SIDE for v in o)

    every = [(z, y, x) for z in range(SIDE) for y in range(SIDE) for x in range(SIDE)]
    every.sort(key=distance)
    alone = [o for o in every if o == negative(o) and o != (0, 0, 0)] + [(0, 0, 0)]
    pairs = list(zip(alone[::2], alone[1::2]))
    seen = set(alone)
    for o in every:
        if o in seen:
            continue
        for turn in (o, (o[1], o[2], o[0]), (o[2], o[0], o[1])):
            if turn not in seen:
                pairs.append((turn, negative(turn)))
                seen.update(pairs[-1])
    pairs.sort(key=lambda p: 99 if (0, 0, 0) in p else distance(p[0]) + distance(p[1]))
    return [(z * SIDE + y) * SIDE + x for pair in pairs for z, y, x in pair]


def packed_offsets():
    codes = send_offsets() + [0]
    return [sum(codes[5 * w + e] << (6 * e) for e in range(5)) for w in range(13)]


def target(j, me):
    word_at = (j * 13) >> 6
    word = jnp.int32(0)
    for index, value in enumerate(packed_offsets()):
        word = jnp.where(word_at == index, jnp.int32(value), word)
    code = word >> (6 * (j - 5 * word_at))
    return (
        ((me & 48) + (code & 48)) & 48
        | ((me & 12) + (code & 12)) & 12
        | ((me & 3) + (code & 3)) & 3
    )


def route_kernel(
    meta,
    length,
    ctx_hbm,
    res_hbm,
    w_hbm,
    down_hbm,
    up_hbm,
    rows_out,
    inner_out,
    lines_out,
    table_out,
    up_v,
    ctx_v,
    res_v,
    w_v,
    down_v,
    lhs,
    own,
    xs,
    xr,
    delta,
    ref_sq,
    pol_sq,
    a_send,
    a_recv,
    a_full,
    s_send,
    s_recv,
    msg,
    line,
    load_sem,
    w_sem,
    xs_sem,
    xr_sem,
    as_sem,
    ar_sem,
    ss_sem,
    sr_sem,
    ms_sem,
    mr_sem,
    small_sem,
):
    me = lax.axis_index("grp")
    tp = lax.axis_index("tp")
    mate = 1 - tp

    barrier = pltpu.get_barrier_semaphore()

    def greet(i, carry):
        pl.semaphore_signal(
            barrier, inc=1, device_id=((me + i) % GROUPS, tp), device_id_type=MESH
        )
        return carry

    loads = [
        pltpu.make_async_copy(ctx_hbm, ctx_v, load_sem.at[0]),
        pltpu.make_async_copy(down_hbm, down_v, load_sem.at[1]),
        pltpu.make_async_copy(up_hbm, up_v, load_sem.at[2]),
        pltpu.make_async_copy(res_hbm, res_v, load_sem.at[3]),
    ]

    def weight_load(c, away):
        half = mate if away else tp
        start = pl.multiple_of(half * HALF + c * CW, CW)
        slot = 2 * (c % WRING) + (0 if away else 1)
        return pltpu.make_async_copy(
            w_hbm.at[:, pl.ds(start, CW)], w_v.at[slot], w_sem.at[slot]
        )

    def mate_copy(src, dst, ssem, rsem):
        return pltpu.make_async_remote_copy(
            src_ref=src,
            dst_ref=dst,
            send_sem=ssem,
            recv_sem=rsem,
            device_id=(me, mate),
            device_id_type=MESH,
        )

    def half_copy(u):
        return mate_copy(xs.at[u % RING], xr.at[u], xs_sem.at[u], xr_sem.at[u])

    def adapter_copy(r):
        return mate_copy(a_send.at[r], a_recv.at[r], as_sem.at[r], ar_sem.at[r])

    def square_copy(r):
        return mate_copy(s_send.at[r], s_recv.at[r], ss_sem.at[r], sr_sem.at[r])

    def far_copy(src, dst, ssem, rsem, there):
        return pltpu.make_async_remote_copy(
            src_ref=src,
            dst_ref=dst,
            send_sem=ssem,
            recv_sem=rsem,
            device_id=(there, tp),
            device_id_type=MESH,
        )

    def start_rows(c, j, there):
        far_copy(
            msg.at[c, j], rows_out.at[c, me], ms_sem.at[c], mr_sem.at[c], there
        ).start()

    def inner_copy(j, there, slot):
        return far_copy(
            a_full.at[j], inner_out.at[slot], small_sem.at[0], small_sem.at[1], there
        )

    def line_copy(j, there, slot):
        return far_copy(line.at[j], lines_out.at[slot], small_sem.at[2], small_sem.at[3], there)

    loads[0].start()
    loads[1].start()
    weight_load(0, True).start()
    weight_load(0, False).start()
    loads[2].start()
    loads[3].start()
    for c in range(1, WRING):
        weight_load(c, True).start()
        weight_load(c, False).start()

    lax.fori_loop(1, GROUPS, greet, 0)
    pl.semaphore_signal(barrier, inc=1, device_id=(me, mate), device_id_type=MESH)

    ref_sq[...] = jnp.zeros_like(ref_sq)
    pol_sq[...] = jnp.zeros_like(pol_sq)
    loads[0].wait()

    def gather(j, carry):
        lhs[j] = ctx_v[meta[0, j]]
        return carry

    lax.fori_loop(0, GROUPS, gather, 0)
    loads[1].wait()

    def squeeze(r, carry):
        at = pl.ds(pl.multiple_of(r * PER, PER), PER)
        a_send[r] = jnp.dot(
            lhs[at].reshape(MB, KDIM), down_v[...], preferred_element_type=jnp.float32
        )
        return carry

    lax.fori_loop(0, NR, squeeze, 0)
    pl.semaphore_wait(barrier, GROUPS)

    def start_adapter(r, carry):
        adapter_copy(r).start()
        return carry

    lax.fori_loop(0, NR, start_adapter, 0)

    lane = lax.broadcasted_iota(jnp.int32, (BLK, RANK), 1)
    token = lax.broadcasted_iota(jnp.int32, (BLK, RANK), 0)

    def unit(u, carry):
        @pl.when(u < UNITS)
        def _():
            c = u // NR
            r = u % NR
            at = pl.ds(pl.multiple_of(r * PER, PER), PER)

            @pl.when(r == 0)
            def _():
                weight_load(c, True).wait()

            @pl.when(u >= RING)
            def _():
                half_copy(u - RING).wait_send()

            xs[u % RING] = jnp.dot(
                lhs[at].reshape(MB, KDIM), w_v[2 * (c % WRING)], preferred_element_type=jnp.float32
            ).astype(jnp.bfloat16)
            half_copy(u).start()

            @pl.when(r == 0)
            def _():
                weight_load(c, False).wait()

            own[u % 2] = jnp.dot(
                lhs[at].reshape(MB, KDIM), w_v[2 * (c % WRING) + 1], preferred_element_type=jnp.float32
            ).astype(jnp.bfloat16)

            @pl.when((r == NR - 1) & (c + WRING < NC))
            def _():
                weight_load(c + WRING, True).start()
                weight_load(c + WRING, False).start()

        @pl.when(u == 1)
        def _():
            def adapt(r, c2):
                adapter_copy(r).wait_recv()
                at = pl.ds(pl.multiple_of(r * PER, PER), PER)
                a_full[at] = (
                    (a_send[r] + a_recv[r]).astype(jnp.bfloat16).reshape(PER, BLK, RANK)
                )
                return c2

            lax.fori_loop(0, NR, adapt, 0)
            loads[2].wait()
            loads[3].wait()

        @pl.when(u >= 1)
        def _():
            v = u - 1
            c = v // NR
            r = v % NR
            at = pl.ds(pl.multiple_of(r * PER, PER), PER)
            cols = pl.ds(pl.multiple_of(c * CW, CW), CW)
            delta[...] = jnp.dot(
                a_full[at].reshape(MB, RANK), up_v[:, cols], preferred_element_type=jnp.float32
            )
            half_copy(v).wait_recv()

            def finish(i0, c2):
                i = i0 + tp * (1 - 2 * (i0 % 2))
                j = r * PER + i
                block = meta[0, j]
                here = pl.ds(pl.multiple_of(i * BLK, BLK), BLK)
                h = (
                    own[v % 2, here, :].astype(jnp.float32)
                    + xr[v, here, :].astype(jnp.float32)
                    + res_v[block, :, cols].astype(jnp.float32)
                )
                msg[c, j] = h.astype(jnp.bfloat16)

                @pl.when(j < GROUPS - 1)
                def _():
                    start_rows(c, j, target(j, me))

                q = h + delta[here, :]
                h2 = h * h
                q2 = q * q
                ref_sum = ref_sq[j]
                pol_sum = pol_sq[j]
                for e in range(CW // RANK):
                    ref_sum = ref_sum + h2[:, e * RANK : (e + 1) * RANK]
                    pol_sum = pol_sum + q2[:, e * RANK : (e + 1) * RANK]
                ref_sq[j] = ref_sum
                pol_sq[j] = pol_sum
                return c2

            lax.fori_loop(0, PER, finish, 0)

        return carry

    lax.fori_loop(0, UNITS + 1, unit, 0)

    wide = lax.broadcasted_iota(jnp.int32, (MB, RANK), 1)

    def start_squares(r, carry):
        at = pl.ds(pl.multiple_of(r * PER, PER), PER)
        s_send[r] = jnp.where(
            wide < RANK // 2,
            jnp.sum(ref_sq[at].reshape(MB, RANK), axis=1, keepdims=True),
            jnp.sum(pol_sq[at].reshape(MB, RANK), axis=1, keepdims=True),
        )
        square_copy(r).start()
        return carry

    lax.fori_loop(0, NR, start_squares, 0)

    def factors(r, carry):
        square_copy(r).wait_recv()

        def one(i, c2):
            j = r * PER + i
            block = meta[0, j]
            here = pl.ds(pl.multiple_of(i * BLK, BLK), BLK)
            total = s_send[r, here, :] + s_recv[r, here, :]
            live = jnp.where(block * BLK + token < length[0], 1.0, 0.0)
            scale = lax.rsqrt(total / FULL + EPSILON) * live
            row = jnp.where(
                lane == token,
                scale[:, 0:1],
                jnp.where(lane == token + BLK, scale[:, RANK // 2 : RANK // 2 + 1], 0.0),
            )
            seat = jnp.where(
                (token == 0) & (lane == 2 * BLK), meta[1, j].astype(jnp.float32), 0.0
            )
            line[j] = jnp.sum(row + seat, axis=0, keepdims=True)

            @pl.when(j < GROUPS - 1)
            def _():
                there = target(j, me)
                inner_copy(j, there, me).start()
                line_copy(j, there, me).start()

            return c2

        lax.fori_loop(0, PER, one, 0)
        return carry

    lax.fori_loop(0, NR, factors, 0)

    last = GROUPS - 1
    keep = [
        pltpu.make_async_copy(msg.at[c, last], rows_out.at[c, me], w_sem.at[c])
        for c in range(NC)
    ]
    keep.append(pltpu.make_async_copy(a_full.at[last], inner_out.at[me], load_sem.at[0]))
    keep.append(pltpu.make_async_copy(line.at[last], lines_out.at[me], load_sem.at[1]))
    for copy in keep:
        copy.start()

    def drain_mate(r, carry):
        adapter_copy(r).wait_send()
        square_copy(r).wait_send()
        return carry

    lax.fori_loop(0, NR, drain_mate, 0)

    def drain_half(u, carry):
        half_copy(u).wait_send()
        return carry

    lax.fori_loop(UNITS - RING, UNITS, drain_half, 0)
    for copy in keep:
        copy.wait()

    others = pl.ds(0, last)
    for at, ref in enumerate((a_full, inner_out, line, lines_out)):
        pltpu.make_async_copy(ref.at[others], ref.at[others], small_sem.at[at]).wait()
    sheet = lines_out[...].reshape(GROUPS, RANK)
    seats = sheet[:, 2 * BLK : 2 * BLK + 1].astype(jnp.int32)
    source = lax.broadcasted_iota(jnp.int32, (GROUPS, RANK), 0)
    place_at = lax.broadcasted_iota(jnp.int32, (GROUPS, RANK), 1)
    table_out[...] = jnp.sum(
        jnp.where(seats == place_at, source, 0), axis=0, keepdims=True
    )
    for c in range(NC):
        sent = msg.at[c, others]
        came = rows_out.at[c, others]
        pltpu.make_async_copy(sent, sent, ms_sem.at[c]).wait()
        pltpu.make_async_copy(came, came, mr_sem.at[c]).wait()


def route(meta, length, context, residual, out_weight, adapter_down, adapter_up):
    any_space = pl.BlockSpec(memory_space=pl.ANY)
    scalars = pl.BlockSpec(memory_space=pltpu.SMEM)
    vector = pl.BlockSpec(memory_space=pltpu.VMEM)
    dma = pltpu.SemaphoreType.DMA
    bf16, f32 = jnp.bfloat16, jnp.float32
    return pl.pallas_call(
        route_kernel,
        out_shape=(
            jax.ShapeDtypeStruct((NC, GROUPS, BLK, CW), bf16),
            jax.ShapeDtypeStruct((GROUPS, BLK, RANK), bf16),
            jax.ShapeDtypeStruct((GROUPS, 1, RANK), f32),
            jax.ShapeDtypeStruct((1, RANK), jnp.int32),
            jax.ShapeDtypeStruct((RANK, HALF), bf16),
        ),
        in_specs=[scalars] * 2 + [any_space] * 5,
        out_specs=(any_space, any_space, vector, vector, vector),
        scratch_shapes=[
            pltpu.VMEM((GROUPS, BLK, KDIM), bf16),
            pltpu.VMEM((GROUPS, BLK, HALF), bf16),
            pltpu.VMEM((2 * WRING, KDIM, CW), bf16),
            pltpu.VMEM((KDIM, RANK), bf16),
            pltpu.VMEM((GROUPS, BLK, KDIM), bf16),
            pltpu.VMEM((2, MB, CW), bf16),
            pltpu.VMEM((RING, MB, CW), bf16),
            pltpu.VMEM((UNITS, MB, CW), bf16),
            pltpu.VMEM((MB, CW), f32),
            pltpu.VMEM((GROUPS, BLK, RANK), f32),
            pltpu.VMEM((GROUPS, BLK, RANK), f32),
            pltpu.VMEM((NR, MB, RANK), f32),
            pltpu.VMEM((NR, MB, RANK), f32),
            pltpu.VMEM((GROUPS, BLK, RANK), bf16),
            pltpu.VMEM((NR, MB, RANK), f32),
            pltpu.VMEM((NR, MB, RANK), f32),
            pltpu.VMEM((NC, GROUPS, BLK, CW), bf16),
            pltpu.VMEM((GROUPS, 1, RANK), f32),
            dma((4,)),
            dma((2 * WRING,)),
            dma((UNITS,)),
            dma((UNITS,)),
            dma((NR,)),
            dma((NR,)),
            dma((NR,)),
            dma((NR,)),
            dma((NC,)),
            dma((NC,)),
            dma((4,)),
        ],
        compiler_params=pltpu.CompilerParams(
            collective_id=0, has_side_effects=True, vmem_limit_bytes=VMEM_LIMIT
        ),
        cost_estimate=pl.CostEstimate(
            flops=2 * ROWS * KDIM * FULL, bytes_accessed=48 * 2**20, transcendentals=0
        ),
        name="route",
    )(
        meta,
        length,
        *[
            pltpu.with_memory_space_constraint(x, pltpu.HBM)
            for x in (context, residual, out_weight, adapter_down, adapter_up)
        ],
    )


VMEM_LIMIT = 44 * 2**20
PLACE_LIMIT = 24 * 2**20
OUT_PER = 8


def place_kernel(table, *refs):
    rows, inner, lines, up, gain, policy, reference, packed = refs
    step = pl.program_id(0)
    lane = lax.broadcasted_iota(jnp.int32, (BLK, RANK), 1)
    token = lax.broadcasted_iota(jnp.int32, (BLK, RANK), 0)
    sources = []
    scales = []
    for e in range(OUT_PER):
        source = table[step * OUT_PER + e]
        packed[e * BLK : (e + 1) * BLK, :] = inner[source]
        row = jnp.broadcast_to(lines[source], (BLK, RANK))
        sources.append(source)
        scales.append(
            (
                jnp.sum(jnp.where(lane == token, row, 0.0), axis=1, keepdims=True),
                jnp.sum(jnp.where(lane == token + BLK, row, 0.0), axis=1, keepdims=True),
            )
        )
    for c in range(NC):
        cols = slice(c * CW, (c + 1) * CW)
        delta = jnp.dot(packed[...], up[:, cols], preferred_element_type=jnp.float32)
        for e in range(OUT_PER):
            at = slice(e * BLK, (e + 1) * BLK)
            ref_scale, pol_scale = scales[e]
            h = rows[c, sources[e]].astype(jnp.float32)
            reference[at, cols] = (h * ref_scale * gain[:, cols]).astype(jnp.bfloat16)
            policy[at, cols] = ((h + delta[at, :]) * pol_scale * gain[:, cols]).astype(
                jnp.bfloat16
            )


def place(table, rows, inner, lines, adapter_up, gain):
    vector = pl.BlockSpec(memory_space=pltpu.VMEM)
    out_spec = pl.BlockSpec((OUT_PER * BLK, HALF), lambda i, table: (i, 0))
    return pl.pallas_call(
        place_kernel,
        grid_spec=pltpu.PrefetchScalarGridSpec(
            num_scalar_prefetch=1,
            grid=(GROUPS // OUT_PER,),
            in_specs=[vector] * 5,
            out_specs=[out_spec, out_spec],
            scratch_shapes=[pltpu.VMEM((OUT_PER * BLK, RANK), jnp.bfloat16)],
        ),
        out_shape=[jax.ShapeDtypeStruct((ROWS, HALF), jnp.bfloat16)] * 2,
        compiler_params=pltpu.CompilerParams(vmem_limit_bytes=PLACE_LIMIT),
        name="place",
    )(table, rows, inner, lines, adapter_up, gain)


def local(
    context,
    residual,
    out_weight,
    adapter_down,
    adapter_up,
    norm_gain,
    lengths,
    route_group,
    route_slot,
):
    position = jnp.arange(GROUPS, dtype=jnp.int32)
    targets = target(position, lax.axis_index("grp"))
    chosen = route_group[0][None, :] == targets[:, None]
    facts = jnp.stack([position, route_slot[0]])
    meta = jnp.sum(jnp.where(chosen[None], facts[:, None, :], 0), axis=2).astype(jnp.int32)
    rows, inner, lines, table, up = route(
        meta,
        lengths,
        context.reshape(GROUPS, BLK, KDIM),
        residual.reshape(GROUPS, BLK, HALF),
        out_weight,
        adapter_down,
        adapter_up,
    )
    return tuple(place(table[0], rows, inner, lines, up, norm_gain[None, :]))


def solution(mesh):
    in_specs = (
        P("grp", "tp"),
        P("grp", "tp"),
        P("tp", None),
        P("tp", None),
        P(None, "tp"),
        P("tp"),
        P("grp"),
        P("grp", None),
        P("grp", None),
    )
    out_specs = (P("grp", "tp"), P("grp", "tp"))
    return jax.shard_map(local, mesh=mesh, in_specs=in_specs, out_specs=out_specs, check_vma=False)
```

```python
import functools

import jax
import jax.numpy as jnp
from jax import lax
from jax.experimental import pallas as pl
from jax.experimental.pallas import tpu as pltpu
from jax.sharding import PartitionSpec as P

EPSILON = 1e-05
MESH = pl.DeviceIdType.MESH

GROUPS = 64
SIDE = 4
BLK = 16
ROWS = 1024
KDIM = 1536
HALF = 3072
FULL = 6144
RANK = 128
PER = 16
MB = PER * BLK
NR = GROUPS // PER
CW = 512
NC = HALF // CW
UNITS = NC * NR
RING = 4
HALF_STEPS = GROUPS // 2
WRING = 4


def target(j, me):
    code = ((j + 1) * 27) & 63
    return (
        ((me & 48) + (code & 48)) & 48
        | ((me & 12) + (code & 12)) & 12
        | ((me & 3) + (code & 3)) & 3
    )


def route_kernel(
    blocks,
    seats_for,
    length,
    ctx_hbm,
    res_hbm,
    w_hbm,
    down_hbm,
    up_hbm,
    rows_out,
    inner_out,
    lines_out,
    table_out,
    up_v,
    ctx_v,
    res_v,
    w_v,
    down_v,
    lhs,
    own,
    xs,
    xr,
    delta,
    ref_sq,
    pol_sq,
    a_send,
    a_recv,
    a_full,
    s_send,
    s_recv,
    msg,
    line,
    load_sem,
    w_sem,
    xs_sem,
    xr_sem,
    as_sem,
    ar_sem,
    ss_sem,
    sr_sem,
    ms_sem,
    mr_sem,
    small_sem,
):
    me = lax.axis_index("grp")
    tp = lax.axis_index("tp")
    mate = 1 - tp

    barrier = pltpu.get_barrier_semaphore()

    def greet(i, carry):
        pl.semaphore_signal(
            barrier, inc=1, device_id=((me + i) % GROUPS, tp), device_id_type=MESH
        )
        return carry

    loads = [
        pltpu.make_async_copy(ctx_hbm, ctx_v, load_sem.at[0]),
        pltpu.make_async_copy(down_hbm, down_v, load_sem.at[1]),
        pltpu.make_async_copy(up_hbm, up_v, load_sem.at[2]),
        pltpu.make_async_copy(res_hbm, res_v, load_sem.at[3]),
    ]

    def weight_load(c, away):
        half = mate if away else tp
        start = pl.multiple_of(half * HALF + c * CW, CW)
        slot = 2 * (c % WRING) + (0 if away else 1)
        return pltpu.make_async_copy(
            w_hbm.at[:, pl.ds(start, CW)], w_v.at[slot], w_sem.at[slot]
        )

    def mate_copy(src, dst, ssem, rsem):
        return pltpu.make_async_remote_copy(
            src_ref=src,
            dst_ref=dst,
            send_sem=ssem,
            recv_sem=rsem,
            device_id=(me, mate),
            device_id_type=MESH,
        )

    def half_copy(u):
        return mate_copy(xs.at[u % RING], xr.at[u], xs_sem.at[u], xr_sem.at[u])

    def adapter_copy(r):
        return mate_copy(a_send.at[r], a_recv.at[r], as_sem.at[r], ar_sem.at[r])

    def square_copy(r):
        return mate_copy(s_send.at[r], s_recv.at[r], ss_sem.at[r], sr_sem.at[r])

    def far_copy(src, dst, ssem, rsem, there):
        return pltpu.make_async_remote_copy(
            src_ref=src,
            dst_ref=dst,
            send_sem=ssem,
            recv_sem=rsem,
            device_id=(there, tp),
            device_id_type=MESH,
        )

    def start_rows(c, j, there):
        far_copy(
            msg.at[c, j], rows_out.at[c, j], ms_sem.at[c], mr_sem.at[c], there
        ).start()

    def inner_copy(j, there):
        return far_copy(a_full.at[j], inner_out.at[j], small_sem.at[0], small_sem.at[1], there)

    def line_copy(j, there):
        return far_copy(line.at[j], lines_out.at[j], small_sem.at[2], small_sem.at[3], there)

    def swap_copy():
        mine = pl.ds(pl.multiple_of(tp * HALF_STEPS, HALF_STEPS), HALF_STEPS)
        return mate_copy(inner_out.at[mine], inner_out.at[mine], small_sem.at[4], small_sem.at[5])

    loads[0].start()
    loads[1].start()
    weight_load(0, True).start()
    weight_load(0, False).start()
    loads[2].start()
    loads[3].start()
    for c in range(1, WRING):
        weight_load(c, True).start()
        weight_load(c, False).start()

    lax.fori_loop(1, GROUPS, greet, 0)
    pl.semaphore_signal(barrier, inc=1, device_id=(me, mate), device_id_type=MESH)

    ref_sq[...] = jnp.zeros_like(ref_sq)
    pol_sq[...] = jnp.zeros_like(pol_sq)
    loads[0].wait()

    def gather(j, carry):
        lhs[j] = ctx_v[blocks[j]]
        return carry

    lax.fori_loop(0, GROUPS, gather, 0)
    loads[1].wait()

    def squeeze(r, carry):
        at = pl.ds(pl.multiple_of(r * PER, PER), PER)
        a_send[r] = jnp.dot(
            lhs[at].reshape(MB, KDIM), down_v[...], preferred_element_type=jnp.float32
        )
        return carry

    lax.fori_loop(0, NR, squeeze, 0)
    pl.semaphore_wait(barrier, GROUPS)

    def start_adapter(r, carry):
        adapter_copy(r).start()
        return carry

    lax.fori_loop(0, NR, start_adapter, 0)

    lane = lax.broadcasted_iota(jnp.int32, (BLK, RANK), 1)
    token = lax.broadcasted_iota(jnp.int32, (BLK, RANK), 0)

    def unit(u, carry):
        @pl.when(u < UNITS)
        def _():
            c = u // NR
            r = u % NR
            at = pl.ds(pl.multiple_of(r * PER, PER), PER)

            @pl.when(r == 0)
            def _():
                weight_load(c, True).wait()

            @pl.when(u >= RING)
            def _():
                half_copy(u - RING).wait_send()

            xs[u % RING] = jnp.dot(
                lhs[at].reshape(MB, KDIM), w_v[2 * (c % WRING)], preferred_element_type=jnp.float32
            ).astype(jnp.bfloat16)
            half_copy(u).start()

            @pl.when(r == 0)
            def _():
                weight_load(c, False).wait()

            own[u % 2] = jnp.dot(
                lhs[at].reshape(MB, KDIM), w_v[2 * (c % WRING) + 1], preferred_element_type=jnp.float32
            ).astype(jnp.bfloat16)

            @pl.when((r == NR - 1) & (c + WRING < NC))
            def _():
                weight_load(c + WRING, True).start()
                weight_load(c + WRING, False).start()

        @pl.when(u == 1)
        def _():
            def adapt(r, c2):
                adapter_copy(r).wait_recv()
                at = pl.ds(pl.multiple_of(r * PER, PER), PER)
                a_full[at] = (
                    (a_send[r] + a_recv[r]).astype(jnp.bfloat16).reshape(PER, BLK, RANK)
                )
                return c2

            lax.fori_loop(0, NR, adapt, 0)
            loads[2].wait()
            loads[3].wait()

        @pl.when(u >= 1)
        def _():
            v = u - 1
            c = v // NR
            r = v % NR
            at = pl.ds(pl.multiple_of(r * PER, PER), PER)
            cols = pl.ds(pl.multiple_of(c * CW, CW), CW)
            delta[...] = jnp.dot(
                a_full[at].reshape(MB, RANK), up_v[:, cols], preferred_element_type=jnp.float32
            )
            half_copy(v).wait_recv()

            def finish(i, c2):
                j = r * PER + i
                block = blocks[j]
                here = pl.ds(pl.multiple_of(i * BLK, BLK), BLK)
                h = (
                    own[v % 2, here, :].astype(jnp.float32)
                    + xr[v, here, :].astype(jnp.float32)
                    + res_v[block, :, cols].astype(jnp.float32)
                )
                msg[c, j] = h.astype(jnp.bfloat16)
                q = h + delta[here, :]
                h2 = h * h
                q2 = q * q
                ref_sum = ref_sq[j]
                pol_sum = pol_sq[j]
                for e in range(CW // RANK):
                    ref_sum = ref_sum + h2[:, e * RANK : (e + 1) * RANK]
                    pol_sum = pol_sum + q2[:, e * RANK : (e + 1) * RANK]
                ref_sq[j] = ref_sum
                pol_sq[j] = pol_sum
                return c2

            lax.fori_loop(0, PER, finish, 0, unroll=4)
            count = PER - r // (NR - 1)

            def post(i, c2):
                j = r * PER + i
                start_rows(c, j, target(j, me))
                return c2

            lax.fori_loop(0, count, post, 0)

            @pl.when((c == 1) & (r // (NR // 2) == tp))
            def _():
                def post_inner(i, c2):
                    j = r * PER + i
                    inner_copy(j, target(j, me)).start()
                    return c2

                lax.fori_loop(0, count, post_inner, 0)

        return carry

    lax.fori_loop(0, UNITS + 1, unit, 0)

    wide = lax.broadcasted_iota(jnp.int32, (MB, RANK), 1)

    def start_squares(r, carry):
        at = pl.ds(pl.multiple_of(r * PER, PER), PER)
        s_send[r] = jnp.where(
            wide < RANK // 2,
            jnp.sum(ref_sq[at].reshape(MB, RANK), axis=1, keepdims=True),
            jnp.sum(pol_sq[at].reshape(MB, RANK), axis=1, keepdims=True),
        )
        square_copy(r).start()
        return carry

    lax.fori_loop(0, NR, start_squares, 0)

    def factors(r, carry):
        square_copy(r).wait_recv()

        def one(i, c2):
            j = r * PER + i
            block = blocks[j]
            here = pl.ds(pl.multiple_of(i * BLK, BLK), BLK)
            total = s_send[r, here, :] + s_recv[r, here, :]
            live = jnp.where(block * BLK + token < length[0], 1.0, 0.0)
            scale = lax.rsqrt(total / FULL + EPSILON) * live
            row = jnp.where(
                lane == token,
                scale[:, 0:1],
                jnp.where(lane == token + BLK, scale[:, RANK // 2 : RANK // 2 + 1], 0.0),
            )
            seat = jnp.where(
                (token == 0) & (lane == 2 * BLK), seats_for[j].astype(jnp.float32), 0.0
            )
            line[j] = jnp.sum(row + seat, axis=0, keepdims=True)

            @pl.when(j < GROUPS - 1)
            def _():
                line_copy(j, target(j, me)).start()

            return c2

        lax.fori_loop(0, PER, one, 0)
        return carry

    lax.fori_loop(0, NR, factors, 0)

    last = GROUPS - 1
    keep = [
        pltpu.make_async_copy(msg.at[c, last], rows_out.at[c, last], w_sem.at[c])
        for c in range(NC)
    ]
    keep.append(pltpu.make_async_copy(line.at[last], lines_out.at[last], load_sem.at[1]))
    for copy in keep:
        copy.start()

    def take_inner(first, count):
        steps = pl.ds(first, count)
        for at, ref in enumerate((a_full, inner_out)):
            pltpu.make_async_copy(ref.at[steps], ref.at[steps], small_sem.at[at]).wait()

    @pl.when(tp == 0)
    def _():
        take_inner(0, HALF_STEPS)

    @pl.when(tp == 1)
    def _():
        own_inner = pltpu.make_async_copy(a_full.at[last], inner_out.at[last], load_sem.at[0])
        own_inner.start()
        take_inner(HALF_STEPS, HALF_STEPS - 1)
        own_inner.wait()

    swap_copy().start()

    def drain_mate(r, carry):
        adapter_copy(r).wait_send()
        square_copy(r).wait_send()
        return carry

    lax.fori_loop(0, NR, drain_mate, 0)

    def drain_half(u, carry):
        half_copy(u).wait_send()
        return carry

    lax.fori_loop(UNITS - RING, UNITS, drain_half, 0)
    for copy in keep:
        copy.wait()

    others = pl.ds(0, last)
    swap_copy().wait()
    for at, ref in ((2, line), (3, lines_out)):
        pltpu.make_async_copy(ref.at[others], ref.at[others], small_sem.at[at]).wait()
    sheet = lines_out[...].reshape(GROUPS, RANK)
    seats = sheet[:, 2 * BLK : 2 * BLK + 1].astype(jnp.int32)
    source = lax.broadcasted_iota(jnp.int32, (GROUPS, RANK), 0)
    place_at = lax.broadcasted_iota(jnp.int32, (GROUPS, RANK), 1)
    table_out[...] = jnp.sum(
        jnp.where(seats == place_at, source, 0), axis=0, keepdims=True
    )
    for c in range(NC):
        sent = msg.at[c, others]
        came = rows_out.at[c, others]
        pltpu.make_async_copy(sent, sent, ms_sem.at[c]).wait()
        pltpu.make_async_copy(came, came, mr_sem.at[c]).wait()


def route(blocks, seats_for, length, context, residual, out_weight, adapter_down, adapter_up):
    any_space = pl.BlockSpec(memory_space=pl.ANY)
    scalars = pl.BlockSpec(memory_space=pltpu.SMEM)
    vector = pl.BlockSpec(memory_space=pltpu.VMEM)
    dma = pltpu.SemaphoreType.DMA
    bf16, f32 = jnp.bfloat16, jnp.float32
    return pl.pallas_call(
        route_kernel,
        out_shape=(
            jax.ShapeDtypeStruct((NC, GROUPS, BLK, CW), bf16),
            jax.ShapeDtypeStruct((GROUPS, BLK, RANK), bf16),
            jax.ShapeDtypeStruct((GROUPS, 1, RANK), f32),
            jax.ShapeDtypeStruct((1, RANK), jnp.int32),
            jax.ShapeDtypeStruct((RANK, HALF), bf16),
        ),
        in_specs=[scalars] * 3 + [any_space] * 5,
        out_specs=(any_space, any_space, vector, vector, vector),
        scratch_shapes=[
            pltpu.VMEM((GROUPS, BLK, KDIM), bf16),
            pltpu.VMEM((GROUPS, BLK, HALF), bf16),
            pltpu.VMEM((2 * WRING, KDIM, CW), bf16),
            pltpu.VMEM((KDIM, RANK), bf16),
            pltpu.VMEM((GROUPS, BLK, KDIM), bf16),
            pltpu.VMEM((2, MB, CW), bf16),
            pltpu.VMEM((RING, MB, CW), bf16),
            pltpu.VMEM((UNITS, MB, CW), bf16),
            pltpu.VMEM((MB, CW), f32),
            pltpu.VMEM((GROUPS, BLK, RANK), f32),
            pltpu.VMEM((GROUPS, BLK, RANK), f32),
            pltpu.VMEM((NR, MB, RANK), f32),
            pltpu.VMEM((NR, MB, RANK), f32),
            pltpu.VMEM((GROUPS, BLK, RANK), bf16),
            pltpu.VMEM((NR, MB, RANK), f32),
            pltpu.VMEM((NR, MB, RANK), f32),
            pltpu.VMEM((NC, GROUPS, BLK, CW), bf16),
            pltpu.VMEM((GROUPS, 1, RANK), f32),
            dma((4,)),
            dma((2 * WRING,)),
            dma((UNITS,)),
            dma((UNITS,)),
            dma((NR,)),
            dma((NR,)),
            dma((NR,)),
            dma((NR,)),
            dma((NC,)),
            dma((NC,)),
            dma((6,)),
        ],
        compiler_params=pltpu.CompilerParams(
            collective_id=0, has_side_effects=True, vmem_limit_bytes=VMEM_LIMIT
        ),
        cost_estimate=pl.CostEstimate(
            flops=2 * ROWS * KDIM * FULL, bytes_accessed=48 * 2**20, transcendentals=0
        ),
        name="route",
    )(
        blocks,
        seats_for,
        length,
        *[
            pltpu.with_memory_space_constraint(x, pltpu.HBM)
            for x in (context, residual, out_weight, adapter_down, adapter_up)
        ],
    )


VMEM_LIMIT = 44 * 2**20
PLACE_LIMIT = 24 * 2**20
OUT_PER = 16


def place_kernel(table, *refs):
    rows, inner, lines, up, gain, policy, reference, packed = refs
    step = pl.program_id(0)
    lane = lax.broadcasted_iota(jnp.int32, (BLK, RANK), 1)
    token = lax.broadcasted_iota(jnp.int32, (BLK, RANK), 0)
    sources = []
    scales = []
    for e in range(OUT_PER):
        source = table[step * OUT_PER + e]
        packed[e * BLK : (e + 1) * BLK, :] = inner[source]
        row = jnp.broadcast_to(lines[source], (BLK, RANK))
        sources.append(source)
        scales.append(
            (
                jnp.sum(jnp.where(lane == token, row, 0.0), axis=1, keepdims=True),
                jnp.sum(jnp.where(lane == token + BLK, row, 0.0), axis=1, keepdims=True),
            )
        )
    for c in range(NC):
        cols = slice(c * CW, (c + 1) * CW)
        delta = jnp.dot(packed[...], up[:, cols], preferred_element_type=jnp.float32)
        for e in range(OUT_PER):
            at = slice(e * BLK, (e + 1) * BLK)
            ref_scale, pol_scale = scales[e]
            h = rows[c, sources[e]].astype(jnp.float32)
            reference[at, cols] = (h * ref_scale * gain[:, cols]).astype(jnp.bfloat16)
            policy[at, cols] = ((h + delta[at, :]) * pol_scale * gain[:, cols]).astype(
                jnp.bfloat16
            )


def place(table, rows, inner, lines, adapter_up, gain):
    vector = pl.BlockSpec(memory_space=pltpu.VMEM)
    out_spec = pl.BlockSpec((OUT_PER * BLK, HALF), lambda i, table: (i, 0))
    return pl.pallas_call(
        place_kernel,
        grid_spec=pltpu.PrefetchScalarGridSpec(
            num_scalar_prefetch=1,
            grid=(GROUPS // OUT_PER,),
            in_specs=[vector] * 5,
            out_specs=[out_spec, out_spec],
            scratch_shapes=[pltpu.VMEM((OUT_PER * BLK, RANK), jnp.bfloat16)],
        ),
        out_shape=[jax.ShapeDtypeStruct((ROWS, HALF), jnp.bfloat16)] * 2,
        compiler_params=pltpu.CompilerParams(vmem_limit_bytes=PLACE_LIMIT),
        name="place",
    )(table, rows, inner, lines, adapter_up, gain)


def local(
    context,
    residual,
    out_weight,
    adapter_down,
    adapter_up,
    norm_gain,
    lengths,
    route_group,
    route_slot,
):
    position = jnp.arange(GROUPS, dtype=jnp.int32)
    targets = target(position, lax.axis_index("grp"))
    chosen = route_group[0][None, :] == targets[:, None]
    blocks = jnp.sum(jnp.where(chosen, position[None, :], 0), axis=1).astype(jnp.int32)
    seats_for = jnp.sum(jnp.where(chosen, route_slot[0][None, :], 0), axis=1).astype(jnp.int32)
    rows, inner, lines, table, up = route(
        blocks,
        seats_for,
        lengths,
        context.reshape(GROUPS, BLK, KDIM),
        residual.reshape(GROUPS, BLK, HALF),
        out_weight,
        adapter_down,
        adapter_up,
    )
    return tuple(place(table[0], rows, inner, lines, up, norm_gain[None, :]))


def solution(mesh):
    in_specs = (
        P("grp", "tp"),
        P("grp", "tp"),
        P("tp", None),
        P("tp", None),
        P(None, "tp"),
        P("tp"),
        P("grp"),
        P("grp", None),
        P("grp", None),
    )
    out_specs = (P("grp", "tp"), P("grp", "tp"))
    return jax.shard_map(local, mesh=mesh, in_specs=in_specs, out_specs=out_specs, check_vma=False)
```

```python
import functools

import jax
import jax.numpy as jnp
from jax import lax
from jax.experimental import pallas as pl
from jax.experimental.pallas import tpu as pltpu
from jax.sharding import PartitionSpec as P

EPSILON = 1e-05
MESH = pl.DeviceIdType.MESH

GROUPS = 64
SIDE = 4
BLK = 16
ROWS = 1024
KDIM = 1536
HALF = 3072
FULL = 6144
RANK = 128
PER = 16
MB = PER * BLK
NR = GROUPS // PER
CW = 512
NC = HALF // CW
UNITS = NC * NR
RING = 4
HALF_STEPS = GROUPS // 2
WRING = 4


def target(j, me):
    code = ((j + 1) * 27) & 63
    return (
        ((me & 48) + (code & 48)) & 48
        | ((me & 12) + (code & 12)) & 12
        | ((me & 3) + (code & 3)) & 3
    )


def route_kernel(
    blocks,
    seats_for,
    length,
    ctx_hbm,
    res_hbm,
    w_hbm,
    down_hbm,
    up_hbm,
    rows_out,
    inner_out,
    lines_out,
    table_out,
    up_v,
    ctx_v,
    res_v,
    w_v,
    down_v,
    lhs,
    own,
    xs,
    xr,
    delta,
    ref_sq,
    pol_sq,
    a_send,
    a_recv,
    a_full,
    s_send,
    s_recv,
    msg,
    line,
    load_sem,
    w_sem,
    xs_sem,
    xr_sem,
    as_sem,
    ar_sem,
    ss_sem,
    sr_sem,
    ms_sem,
    mr_sem,
    small_sem,
):
    me = lax.axis_index("grp")
    tp = lax.axis_index("tp")
    mate = 1 - tp

    barrier = pltpu.get_barrier_semaphore()

    def greet(i, carry):
        pl.semaphore_signal(
            barrier, inc=1, device_id=((me + i) % GROUPS, tp), device_id_type=MESH
        )
        return carry

    loads = [
        pltpu.make_async_copy(ctx_hbm, ctx_v, load_sem.at[0]),
        pltpu.make_async_copy(down_hbm, down_v, load_sem.at[1]),
        pltpu.make_async_copy(up_hbm, up_v, load_sem.at[2]),
        pltpu.make_async_copy(res_hbm, res_v, load_sem.at[3]),
    ]

    def weight_load(c, away):
        half = mate if away else tp
        start = pl.multiple_of(half * HALF + c * CW, CW)
        slot = 2 * (c % WRING) + (0 if away else 1)
        return pltpu.make_async_copy(
            w_hbm.at[:, pl.ds(start, CW)], w_v.at[slot], w_sem.at[slot]
        )

    def mate_copy(src, dst, ssem, rsem):
        return pltpu.make_async_remote_copy(
            src_ref=src,
            dst_ref=dst,
            send_sem=ssem,
            recv_sem=rsem,
            device_id=(me, mate),
            device_id_type=MESH,
        )

    def half_copy(u):
        return mate_copy(xs.at[u % RING], xr.at[u], xs_sem.at[u], xr_sem.at[u])

    def adapter_copy(r):
        return mate_copy(a_send.at[r], a_recv.at[r], as_sem.at[r], ar_sem.at[r])

    def square_copy(r):
        return mate_copy(s_send.at[r], s_recv.at[r], ss_sem.at[r], sr_sem.at[r])

    def far_copy(src, dst, ssem, rsem, there):
        return pltpu.make_async_remote_copy(
            src_ref=src,
            dst_ref=dst,
            send_sem=ssem,
            recv_sem=rsem,
            device_id=(there, tp),
            device_id_type=MESH,
        )

    def start_rows(c, j, there):
        far_copy(
            msg.at[c, j], rows_out.at[c, j], ms_sem.at[c], mr_sem.at[c], there
        ).start()

    def inner_copy(j, there):
        return far_copy(a_full.at[j], inner_out.at[j], small_sem.at[0], small_sem.at[1], there)

    def line_copy(j, there):
        return far_copy(line.at[j], lines_out.at[j], small_sem.at[2], small_sem.at[3], there)

    def swap_copy():
        mine = pl.ds(pl.multiple_of(tp * HALF_STEPS, HALF_STEPS), HALF_STEPS)
        return mate_copy(inner_out.at[mine], inner_out.at[mine], small_sem.at[4], small_sem.at[5])

    loads[0].start()
    loads[1].start()
    weight_load(0, True).start()
    weight_load(0, False).start()
    loads[2].start()
    loads[3].start()

    lax.fori_loop(1, GROUPS, greet, 0)
    pl.semaphore_signal(barrier, inc=1, device_id=(me, mate), device_id_type=MESH)

    ref_sq[...] = jnp.zeros_like(ref_sq)
    pol_sq[...] = jnp.zeros_like(pol_sq)
    loads[0].wait()

    def gather(j, carry):
        lhs[j] = ctx_v[blocks[j]]
        return carry

    lax.fori_loop(0, GROUPS, gather, 0)
    loads[1].wait()

    def squeeze(r, carry):
        at = pl.ds(pl.multiple_of(r * PER, PER), PER)
        a_send[r] = jnp.dot(
            lhs[at].reshape(MB, KDIM), down_v[...], preferred_element_type=jnp.float32
        )
        return carry

    weight_load(1, True).start()
    weight_load(1, False).start()
    lax.fori_loop(0, NR, squeeze, 0)
    pl.semaphore_wait(barrier, GROUPS)

    def start_adapter(r, carry):
        adapter_copy(r).start()
        return carry

    lax.fori_loop(0, NR, start_adapter, 0)

    lane = lax.broadcasted_iota(jnp.int32, (BLK, RANK), 1)
    token = lax.broadcasted_iota(jnp.int32, (BLK, RANK), 0)

    def unit(u, carry):
        @pl.when(u < UNITS)
        def _():
            c = u // NR
            r = u % NR
            at = pl.ds(pl.multiple_of(r * PER, PER), PER)

            @pl.when(r == 0)
            def _():
                weight_load(c, True).wait()

            @pl.when(u >= RING)
            def _():
                half_copy(u - RING).wait_send()

            xs[u % RING] = jnp.dot(
                lhs[at].reshape(MB, KDIM), w_v[2 * (c % WRING)], preferred_element_type=jnp.float32
            ).astype(jnp.bfloat16)
            half_copy(u).start()

            @pl.when(r == 0)
            def _():
                weight_load(c, False).wait()

            own[u % 2] = jnp.dot(
                lhs[at].reshape(MB, KDIM), w_v[2 * (c % WRING) + 1], preferred_element_type=jnp.float32
            ).astype(jnp.bfloat16)

            @pl.when((r == NR - 1) & (c + WRING < NC))
            def _():
                weight_load(c + WRING, True).start()
                weight_load(c + WRING, False).start()

        @pl.when(u == 1)
        def _():
            def adapt(r, c2):
                adapter_copy(r).wait_recv()
                at = pl.ds(pl.multiple_of(r * PER, PER), PER)
                a_full[at] = (
                    (a_send[r] + a_recv[r]).astype(jnp.bfloat16).reshape(PER, BLK, RANK)
                )
                return c2

            lax.fori_loop(0, NR, adapt, 0)
            loads[2].wait()
            loads[3].wait()
            for later in range(2, WRING):
                weight_load(later, True).start()
                weight_load(later, False).start()

        @pl.when(u >= 1)
        def _():
            v = u - 1
            c = v // NR
            r = v % NR
            at = pl.ds(pl.multiple_of(r * PER, PER), PER)
            cols = pl.ds(pl.multiple_of(c * CW, CW), CW)
            delta[...] = jnp.dot(
                a_full[at].reshape(MB, RANK), up_v[:, cols], preferred_element_type=jnp.float32
            )
            half_copy(v).wait_recv()

            def finish(i, c2):
                j = r * PER + i
                block = blocks[j]
                here = pl.ds(pl.multiple_of(i * BLK, BLK), BLK)
                h = (
                    own[v % 2, here, :].astype(jnp.float32)
                    + xr[v, here, :].astype(jnp.float32)
                    + res_v[block, :, cols].astype(jnp.float32)
                )
                msg[c, j] = h.astype(jnp.bfloat16)
                q = h + delta[here, :]
                h2 = h * h
                q2 = q * q
                ref_sum = ref_sq[j]
                pol_sum = pol_sq[j]
                for e in range(CW // RANK):
                    ref_sum = ref_sum + h2[:, e * RANK : (e + 1) * RANK]
                    pol_sum = pol_sum + q2[:, e * RANK : (e + 1) * RANK]
                ref_sq[j] = ref_sum
                pol_sq[j] = pol_sum
                return c2

            lax.fori_loop(0, PER, finish, 0, unroll=4)
            count = PER - r // (NR - 1)

            def post(i, c2):
                j = r * PER + i
                start_rows(c, j, target(j, me))
                return c2

            lax.fori_loop(0, count, post, 0)

            @pl.when((c == 1) & (r // (NR // 2) == tp))
            def _():
                def post_inner(i, c2):
                    j = r * PER + i
                    inner_copy(j, target(j, me)).start()
                    return c2

                lax.fori_loop(0, count, post_inner, 0)

        return carry

    lax.fori_loop(0, UNITS + 1, unit, 0)

    wide = lax.broadcasted_iota(jnp.int32, (MB, RANK), 1)

    def start_squares(r, carry):
        at = pl.ds(pl.multiple_of(r * PER, PER), PER)
        s_send[r] = jnp.where(
            wide < RANK // 2,
            jnp.sum(ref_sq[at].reshape(MB, RANK), axis=1, keepdims=True),
            jnp.sum(pol_sq[at].reshape(MB, RANK), axis=1, keepdims=True),
        )
        square_copy(r).start()
        return carry

    lax.fori_loop(0, NR, start_squares, 0)

    def factors(r, carry):
        square_copy(r).wait_recv()

        def one(i, c2):
            j = r * PER + i
            block = blocks[j]
            here = pl.ds(pl.multiple_of(i * BLK, BLK), BLK)
            total = s_send[r, here, :] + s_recv[r, here, :]
            live = jnp.where(block * BLK + token < length[0], 1.0, 0.0)
            scale = lax.rsqrt(total / FULL + EPSILON) * live
            row = jnp.where(
                lane == token,
                scale[:, 0:1],
                jnp.where(lane == token + BLK, scale[:, RANK // 2 : RANK // 2 + 1], 0.0),
            )
            seat = jnp.where(
                (token == 0) & (lane == 2 * BLK), seats_for[j].astype(jnp.float32), 0.0
            )
            line[j] = jnp.sum(row + seat, axis=0, keepdims=True)

            @pl.when(j < GROUPS - 1)
            def _():
                line_copy(j, target(j, me)).start()

            return c2

        lax.fori_loop(0, PER, one, 0)
        return carry

    lax.fori_loop(0, NR, factors, 0)

    last = GROUPS - 1
    keep = [
        pltpu.make_async_copy(msg.at[c, last], rows_out.at[c, last], w_sem.at[c])
        for c in range(NC)
    ]
    keep.append(pltpu.make_async_copy(line.at[last], lines_out.at[last], load_sem.at[1]))
    for copy in keep:
        copy.start()

    def take_inner(first, count):
        steps = pl.ds(first, count)
        for at, ref in enumerate((a_full, inner_out)):
            pltpu.make_async_copy(ref.at[steps], ref.at[steps], small_sem.at[at]).wait()

    @pl.when(tp == 0)
    def _():
        take_inner(0, HALF_STEPS)

    @pl.when(tp == 1)
    def _():
        own_inner = pltpu.make_async_copy(a_full.at[last], inner_out.at[last], load_sem.at[0])
        own_inner.start()
        take_inner(HALF_STEPS, HALF_STEPS - 1)
        own_inner.wait()

    swap_copy().start()

    def drain_mate(r, carry):
        adapter_copy(r).wait_send()
        square_copy(r).wait_send()
        return carry

    lax.fori_loop(0, NR, drain_mate, 0)

    def drain_half(u, carry):
        half_copy(u).wait_send()
        return carry

    lax.fori_loop(UNITS - RING, UNITS, drain_half, 0)
    for copy in keep:
        copy.wait()

    others = pl.ds(0, last)
    swap_copy().wait()
    for at, ref in ((2, line), (3, lines_out)):
        pltpu.make_async_copy(ref.at[others], ref.at[others], small_sem.at[at]).wait()
    sheet = lines_out[...].reshape(GROUPS, RANK)
    seats = sheet[:, 2 * BLK : 2 * BLK + 1].astype(jnp.int32)
    source = lax.broadcasted_iota(jnp.int32, (GROUPS, RANK), 0)
    place_at = lax.broadcasted_iota(jnp.int32, (GROUPS, RANK), 1)
    table_out[...] = jnp.sum(
        jnp.where(seats == place_at, source, 0), axis=0, keepdims=True
    )
    for c in range(NC):
        sent = msg.at[c, others]
        came = rows_out.at[c, others]
        pltpu.make_async_copy(sent, sent, ms_sem.at[c]).wait()
        pltpu.make_async_copy(came, came, mr_sem.at[c]).wait()


def route(blocks, seats_for, length, context, residual, out_weight, adapter_down, adapter_up):
    any_space = pl.BlockSpec(memory_space=pl.ANY)
    scalars = pl.BlockSpec(memory_space=pltpu.SMEM)
    vector = pl.BlockSpec(memory_space=pltpu.VMEM)
    dma = pltpu.SemaphoreType.DMA
    bf16, f32 = jnp.bfloat16, jnp.float32
    return pl.pallas_call(
        route_kernel,
        out_shape=(
            jax.ShapeDtypeStruct((NC, GROUPS, BLK, CW), bf16),
            jax.ShapeDtypeStruct((GROUPS, BLK, RANK), bf16),
            jax.ShapeDtypeStruct((GROUPS, 1, RANK), f32),
            jax.ShapeDtypeStruct((1, RANK), jnp.int32),
            jax.ShapeDtypeStruct((RANK, HALF), bf16),
        ),
        in_specs=[scalars] * 3 + [any_space] * 5,
        out_specs=(any_space, any_space, vector, vector, vector),
        scratch_shapes=[
            pltpu.VMEM((GROUPS, BLK, KDIM), bf16),
            pltpu.VMEM((GROUPS, BLK, HALF), bf16),
            pltpu.VMEM((2 * WRING, KDIM, CW), bf16),
            pltpu.VMEM((KDIM, RANK), bf16),
            pltpu.VMEM((GROUPS, BLK, KDIM), bf16),
            pltpu.VMEM((2, MB, CW), bf16),
            pltpu.VMEM((RING, MB, CW), bf16),
            pltpu.VMEM((UNITS, MB, CW), bf16),
            pltpu.VMEM((MB, CW), f32),
            pltpu.VMEM((GROUPS, BLK, RANK), f32),
            pltpu.VMEM((GROUPS, BLK, RANK), f32),
            pltpu.VMEM((NR, MB, RANK), f32),
            pltpu.VMEM((NR, MB, RANK), f32),
            pltpu.VMEM((GROUPS, BLK, RANK), bf16),
            pltpu.VMEM((NR, MB, RANK), f32),
            pltpu.VMEM((NR, MB, RANK), f32),
            pltpu.VMEM((NC, GROUPS, BLK, CW), bf16),
            pltpu.VMEM((GROUPS, 1, RANK), f32),
            dma((4,)),
            dma((2 * WRING,)),
            dma((UNITS,)),
            dma((UNITS,)),
            dma((NR,)),
            dma((NR,)),
            dma((NR,)),
            dma((NR,)),
            dma((NC,)),
            dma((NC,)),
            dma((6,)),
        ],
        compiler_params=pltpu.CompilerParams(
            collective_id=0, has_side_effects=True, vmem_limit_bytes=VMEM_LIMIT
        ),
        cost_estimate=pl.CostEstimate(
            flops=2 * ROWS * KDIM * FULL, bytes_accessed=48 * 2**20, transcendentals=0
        ),
        name="route",
    )(
        blocks,
        seats_for,
        length,
        *[
            pltpu.with_memory_space_constraint(x, pltpu.HBM)
            for x in (context, residual, out_weight, adapter_down, adapter_up)
        ],
    )


VMEM_LIMIT = 44 * 2**20
PLACE_LIMIT = 24 * 2**20
OUT_PER = 16


def place_kernel(table, *refs):
    rows, inner, lines, up, gain, policy, reference, packed = refs
    step = pl.program_id(0)
    lane = lax.broadcasted_iota(jnp.int32, (BLK, RANK), 1)
    token = lax.broadcasted_iota(jnp.int32, (BLK, RANK), 0)
    sources = []
    scales = []
    for e in range(OUT_PER):
        source = table[step * OUT_PER + e]
        packed[e * BLK : (e + 1) * BLK, :] = inner[source]
        row = jnp.broadcast_to(lines[source], (BLK, RANK))
        sources.append(source)
        scales.append(
            (
                jnp.sum(jnp.where(lane == token, row, 0.0), axis=1, keepdims=True),
                jnp.sum(jnp.where(lane == token + BLK, row, 0.0), axis=1, keepdims=True),
            )
        )
    for c in range(NC):
        cols = slice(c * CW, (c + 1) * CW)
        delta = jnp.dot(packed[...], up[:, cols], preferred_element_type=jnp.float32)
        for e in range(OUT_PER):
            at = slice(e * BLK, (e + 1) * BLK)
            ref_scale, pol_scale = scales[e]
            h = rows[c, sources[e]].astype(jnp.float32)
            reference[at, cols] = (h * ref_scale * gain[:, cols]).astype(jnp.bfloat16)
            policy[at, cols] = ((h + delta[at, :]) * pol_scale * gain[:, cols]).astype(
                jnp.bfloat16
            )


def place(table, rows, inner, lines, adapter_up, gain):
    vector = pl.BlockSpec(memory_space=pltpu.VMEM)
    out_spec = pl.BlockSpec((OUT_PER * BLK, HALF), lambda i, table: (i, 0))
    return pl.pallas_call(
        place_kernel,
        grid_spec=pltpu.PrefetchScalarGridSpec(
            num_scalar_prefetch=1,
            grid=(GROUPS // OUT_PER,),
            in_specs=[vector] * 5,
            out_specs=[out_spec, out_spec],
            scratch_shapes=[pltpu.VMEM((OUT_PER * BLK, RANK), jnp.bfloat16)],
        ),
        out_shape=[jax.ShapeDtypeStruct((ROWS, HALF), jnp.bfloat16)] * 2,
        compiler_params=pltpu.CompilerParams(vmem_limit_bytes=PLACE_LIMIT),
        name="place",
    )(table, rows, inner, lines, adapter_up, gain)


def local(
    context,
    residual,
    out_weight,
    adapter_down,
    adapter_up,
    norm_gain,
    lengths,
    route_group,
    route_slot,
):
    position = jnp.arange(GROUPS, dtype=jnp.int32)
    targets = target(position, lax.axis_index("grp"))
    chosen = route_group[0][None, :] == targets[:, None]
    blocks = jnp.sum(jnp.where(chosen, position[None, :], 0), axis=1).astype(jnp.int32)
    seats_for = jnp.sum(jnp.where(chosen, route_slot[0][None, :], 0), axis=1).astype(jnp.int32)
    rows, inner, lines, table, up = route(
        blocks,
        seats_for,
        lengths,
        context.reshape(GROUPS, BLK, KDIM),
        residual.reshape(GROUPS, BLK, HALF),
        out_weight,
        adapter_down,
        adapter_up,
    )
    return tuple(place(table[0], rows, inner, lines, up, norm_gain[None, :]))


def solution(mesh):
    in_specs = (
        P("grp", "tp"),
        P("grp", "tp"),
        P("tp", None),
        P("tp", None),
        P(None, "tp"),
        P("tp"),
        P("grp"),
        P("grp", None),
        P("grp", None),
    )
    out_specs = (P("grp", "tp"), P("grp", "tp"))
    return jax.shard_map(local, mesh=mesh, in_specs=in_specs, out_specs=out_specs, check_vma=False)
```
